768 devices in a mesh: det: 8 (over y), span: 96 (over z, x, core).
Axes of the slice: x: 4, y: 8, z: 12, core: 2. Of those that a mesh axis runs over, the one named last changes fastest.
Arguments:
- amplitudes: float32 [8, 6144], P('det', 'span'), may hold values from -6 to 6
- residual: float32 [8, 6144], P('det', 'span'), may hold values from -6 to 6
- direction: float32 [8, 6144], P('det', 'span'), may hold values from -6 to 6
- pointing: int32 [8, 6144, 4096], P('det', 'span'), may hold values from 0 to 1023
- pol_weights: bfloat16 [2, 8, 6144, 4096], P(None, 'det', 'span'), may hold values from -1 to 1, as said below
- counts: int32 [8, 6144], P('det', 'span'), may hold values from 1024 to 4096
- tile_patch: int32 [8, 6144], P('det', 'span'), may hold values from 0 to 767, as said below
- patch_slot: int32 [768], replicated, may hold values from 0 to 767, as said below
- inv_hits: float32 [6, 786432], P(None, 'det'), as said below
Outputs:
- amplitudes_next: float32 [8, 6144], P('det', 'span')
- residual_next: float32 [8, 6144], P('det', 'span')
- direction_next: float32 [8, 6144], P('det', 'span')
The draws below stay inside these ranges and needn't reach their ends.
Inputs may be any that keep to these rules, and one draw needn't show every extreme that they name: Patch p belongs to detector group patch_slot[p] // 96, at row patch_slot[p] % 96 of that group; every slot is used once. `tile_patch`: of the 64 baselines of one device, at most 16 fall into patches of one owner, and on every device some owner gets exactly 16. `inv_hits`: for each pixel, the six distinct entries of a symmetric positive definite 3x3 matrix. `pol_weights`: cosine and sine of twice a polarization angle.
All inputs are finite; a program needn't handle non-finite values.
Results may differ from the reference program's by a relative error of at most 0.0003.
Values sent between devices are 32-bit elements; how exact they have to be, the bound alone decides.
No kernel may reach another device: no remote copies, remote signals or barrier semaphores. Data moves between devices by JAX's collectives and lax.ppermute only.
A program may use at most 128 MiB of HBM per device.

```python
import math
import jax
import jax.numpy as jnp
from jax import lax

SB = 4096
PP = 1024
NT = 64
POWN = 96
CAP = 16
TILES = 6144
NPATCH = 768
N_DET = 8
N_SPAN = 96


def routing(key):
    slot_order = jax.random.permutation(jax.random.fold_in(key, 11), NPATCH).astype(jnp.int32)
    patch_of_slot = jnp.argsort(slot_order, stable=True).astype(jnp.int32)
    device_count = N_DET * N_SPAN
    key_full, key_order, key_row = jax.random.split(jax.random.fold_in(key, 12), 3)
    full_owner = jax.random.randint(key_full, (device_count, 1), 0, N_DET).astype(jnp.int32)
    position = jnp.arange(NT, dtype=jnp.int32)[None, :]
    spread = (full_owner + 1 + (position - CAP) % (N_DET - 1)) % N_DET
    owners = jnp.where(position < CAP, full_owner, spread)
    shuffle = jax.vmap(lambda subkey: jax.random.permutation(subkey, NT))(jax.random.split(key_order, device_count))
    owners = jnp.take_along_axis(owners, shuffle.astype(jnp.int32), axis=1)
    patch_rows = jax.random.randint(key_row, (device_count, NT), 0, POWN).astype(jnp.int32)
    slots = owners * POWN + patch_rows
    patches = patch_of_slot[slots]
    slot_load = jax.ops.segment_sum(jnp.ones((device_count * NT,), jnp.int32), slots.reshape(-1), num_segments=NPATCH)
    return (slot_order, patches.reshape(N_DET, N_SPAN * NT), slot_load)


def draw_patch_slot(key, part):
    shared = routing(key)
    return shared[0]


def draw_tile_patch(key, part):
    shared = routing(key)
    return shared[1]


def draw_pol_weights(key, part):
    key = jax.random.fold_in(key, 3)
    key_base, key_group, key_turns, key_sign, key_jitter = jax.random.split(key, 5)
    base_angle = jax.random.uniform(key_base, (N_DET, N_SPAN * NT, 1), jnp.float32, -math.pi, math.pi)
    group_offset = 0.05 * jax.random.normal(key_group, (N_DET, 1, 1), jnp.float32)
    turn_count = jax.random.uniform(key_turns, (N_DET, N_SPAN * NT, 1), jnp.float32, 4.0, 16.0)
    turn_sign = jnp.where(jax.random.uniform(key_sign, (N_DET, N_SPAN * NT, 1), jnp.float32) < 0.5, -1.0, 1.0)
    jitter = jax.random.uniform(key_jitter, (N_DET, N_SPAN * NT, SB), jnp.float32, -0.4, 0.4)
    position = jnp.arange(SB, dtype=jnp.float32)[None, None, :] / SB - 0.5
    angle = base_angle + group_offset + turn_sign * turn_count * math.pi * position + jitter
    return jnp.stack([jnp.cos(2.0 * angle), jnp.sin(2.0 * angle)]).astype(jnp.bfloat16)


def draw_inv_hits(key, part):
    slot_load = routing(key)[2]
    key = jax.random.fold_in(key, 4)
    keys = jax.random.split(key, 6)
    valid_hits = jnp.maximum(slot_load, 1).astype(jnp.float32) * (0.625 * SB / PP)
    scale = jnp.repeat(1.0 / valid_hits, PP, total_repeat_length=NPATCH * PP)
    shape = (NPATCH * PP,)
    diag_i = jax.random.uniform(keys[0], shape, jnp.float32, 0.8, 1.25) * scale
    diag_q = jax.random.uniform(keys[1], shape, jnp.float32, 1.6, 2.5) * scale
    diag_u = jax.random.uniform(keys[2], shape, jnp.float32, 1.6, 2.5) * scale
    off_iq = jax.random.uniform(keys[3], shape, jnp.float32, -0.2, 0.2) * jnp.sqrt(diag_i * diag_q)
    off_iu = jax.random.uniform(keys[4], shape, jnp.float32, -0.2, 0.2) * jnp.sqrt(diag_i * diag_u)
    off_qu = jax.random.uniform(keys[5], shape, jnp.float32, -0.2, 0.2) * jnp.sqrt(diag_q * diag_u)
    return jnp.stack([diag_i, off_iq, off_iu, diag_q, off_qu, diag_u]).astype(jnp.float32)


def plant(drawn, rng, smallest, top_value):
    longest = drawn.shape.index(max(drawn.shape))
    spots = []
    for shift in (0, 1):
        where = [jax.random.randint(jax.random.fold_in(rng, axis), (), 0, length) for axis, length in enumerate(drawn.shape)]
        where[longest] = (where[longest] + shift) % drawn.shape[longest]
        spots.append(tuple(where))
    return drawn.at[spots[0]].set(smallest).at[spots[1]].set(top_value)


def steps_of(rng, shape, shards, low, largest):
    def one(axis_at, shards_of):
        draws = jax.random.uniform(jax.random.fold_in(jax.random.fold_in(rng, 6), axis_at), (shards_of,), jnp.float32, low / len(shards), largest / len(shards))
        return jnp.repeat(jnp.exp(draws), shape[axis_at] // shards_of).reshape((-1,) + (1,) * (len(shape) - axis_at - 1))

    gain = one(*shards[0])
    for cut in shards[1:]:
        gain = gain * one(*cut)
    return gain


def gaussian(stream_key, dims, width, limit, cuts=(), kind=jnp.bfloat16):
    array = jax.random.normal(stream_key, dims, jnp.float32) * width
    if len(cuts) > 0:
        array = steps_of(stream_key, dims, cuts, -0.22, 0.18) * array
    return jnp.clip(array, min=-limit, max=limit).astype(kind)


def setup_inputs(seed: int = 0) -> dict:
    key_list = jax.random.split(jax.random.key(seed), 10)
    amplitudes = gaussian(key_list[0], (N_DET, TILES), 1.0, 6.0, ((0, 8), (1, 96)), jnp.float32)
    residual = gaussian(key_list[1], (N_DET, TILES), 1.0, 6.0, ((0, 8), (1, 96)), jnp.float32)
    direction = gaussian(key_list[2], (N_DET, TILES), 1.0, 6.0, ((0, 8), (1, 96)), jnp.float32)
    pointing = plant(jax.random.randint(key_list[3], (N_DET, TILES, SB), 0, PP), jax.random.fold_in(key_list[3], 1), 0, PP - 1).astype(jnp.int32)
    pol_weights = draw_pol_weights(jax.random.fold_in(key_list[9], 71), 0)
    counts = plant(jax.random.randint(key_list[5], (N_DET, TILES), SB // 4, SB + 1), jax.random.fold_in(key_list[5], 1), SB // 4, SB).astype(jnp.int32)
    tile_patch = draw_tile_patch(jax.random.fold_in(key_list[9], 71), 0)
    patch_slot = draw_patch_slot(jax.random.fold_in(key_list[9], 71), 0)
    inv_hits = draw_inv_hits(jax.random.fold_in(key_list[9], 71), 0)
    return dict(amplitudes=amplitudes, residual=residual, direction=direction, pointing=pointing, pol_weights=pol_weights, counts=counts, tile_patch=tile_patch, patch_slot=patch_slot, inv_hits=inv_hits)


def apply_inverse(inverse, first, second, third):
    return (inverse[0] * first + inverse[1] * second + inverse[2] * third,
            inverse[1] * first + inverse[3] * second + inverse[4] * third,
            inverse[2] * first + inverse[4] * second + inverse[5] * third)


def patch_counts(pointing, pol_weights, counts):
    tile_count = pointing.shape[1]

    def one_group(inputs):
        pixel_index, cos_part, sin_part, group_counts = inputs
        valid_mask = (lax.broadcasted_iota(jnp.int32, pixel_index.shape, 1) < group_counts[:, None]).astype(jnp.float32)
        segment_ids = (jnp.arange(tile_count, dtype=jnp.int32)[:, None] * PP + pixel_index).reshape(-1)
        weighted = [valid_mask, cos_part.astype(jnp.float32) * valid_mask, sin_part.astype(jnp.float32) * valid_mask]
        binned_parts = [jax.ops.segment_sum(value.reshape(-1), segment_ids, num_segments=tile_count * PP).reshape(tile_count, PP) for value in weighted]
        return jnp.stack(binned_parts, axis=1)

    return lax.map(one_group, (pointing, pol_weights[0], pol_weights[1], counts))


def reference(amplitudes, residual, direction, pointing, pol_weights, counts, tile_patch, patch_slot, inv_hits):
    tile_hits = patch_counts(pointing, pol_weights, counts)
    tile_slots = patch_slot[tile_patch]
    det_count, tile_count = tile_slots.shape
    weighted_hits = tile_hits.reshape(det_count * tile_count, 3, PP) * direction.reshape(-1)[:, None, None]
    binned = jax.ops.segment_sum(weighted_hits, tile_slots.reshape(-1), num_segments=NPATCH)
    inverse = inv_hits.reshape(6, NPATCH, PP)
    mapped = jnp.stack(apply_inverse(inverse, binned[:, 0], binned[:, 1], binned[:, 2]), axis=1)

    def group_terms(inputs):
        group_hits, group_slots = inputs
        return jnp.sum(group_hits * mapped[group_slots], axis=(1, 2))

    correction = lax.map(group_terms, (tile_hits, tile_slots))
    tile_counts = counts.astype(jnp.float32)
    image = (tile_counts * direction - correction) / SB
    scaled = SB * residual / tile_counts
    res_norm = jnp.sum(residual * scaled)
    curvature = jnp.sum(direction * image)
    step_size = res_norm / curvature
    amplitudes_next = amplitudes + step_size * direction
    residual_next = residual - step_size * image
    scaled_next = SB * residual_next / tile_counts
    norm_next = jnp.sum(residual_next * scaled_next)
    direction_next = scaled_next + (norm_next / res_norm) * direction
    return amplitudes_next, residual_next, direction_next
```

```python
import functools
import jax
import jax.numpy as jnp
from jax import lax
from jax.experimental import pallas as pl
from jax.experimental.pallas import tpu as pltpu
from jax.sharding import Mesh, PartitionSpec as P

SB = 4096
PP = 1024
NT = 64
POWN = 96
CAP = 16
NPATCH = 768
NZ = 12
ROWS = POWN // NZ
GROUP = ("det", "x", "c")
PEERS = 64
BF = jnp.bfloat16
F32 = jnp.float32
NT_DIMS = (((1,), (1,)), ((), ()))
VMEM = pl.BlockSpec(memory_space=pltpu.VMEM)
SMEM = pl.BlockSpec(memory_space=pltpu.SMEM)
PARAMS = pltpu.CompilerParams(vmem_limit_bytes=32 * 2**20)


def shape(*dims, dtype=F32):
    return jax.ShapeDtypeStruct(dims, dtype)


def iota(dims, axis):
    return lax.broadcasted_iota(jnp.int32, dims, axis)


def pieces(value):
    first = value.astype(BF)
    rest = value - first.astype(F32)
    second = rest.astype(BF)
    third = (rest - second.astype(F32)).astype(BF)
    return first, second, third


def dot(left, right):
    return jnp.dot(left, right, preferred_element_type=F32)


def dot_t(left, right):
    return lax.dot_general(left, right, NT_DIMS, preferred_element_type=F32)


def route_kernel(patch_ref, slot_ref, dir_ref, codes_ref, place_ref):
    patch = patch_ref[...]
    slots = slot_ref[...]
    patch_hot = (iota((NPATCH, NT), 0) == patch).astype(F32).astype(BF)
    line = iota((8, NPATCH), 0)
    digits = jnp.where(line == 0, slots >> 5, jnp.where(line == 1, slots & 31, 0))
    found = dot(digits.astype(F32).astype(BF), patch_hot)
    slot = (32.0 * found[0:1] + found[1:2]).astype(jnp.int32)
    owner = (slot * 683) >> 16
    row = slot - POWN * owner
    owner_hot = iota((8, NT), 0) == owner
    hot = owner_hot.astype(F32)
    earlier = (iota((NT, NT), 0) < iota((NT, NT), 1)).astype(F32).astype(BF)
    queue = dot(hot.astype(BF), earlier)
    rank = jnp.sum(hot * queue, axis=0, keepdims=True).astype(jnp.int32)
    lane = iota((128, NT), 0)
    at_code = (lane == rank).astype(F32).astype(BF)
    at_dir = (lane == rank + CAP).astype(F32).astype(BF)
    codes = dot_t((hot * (row + 1).astype(F32)).astype(BF), at_code)
    first, second, third = pieces(hot * dir_ref[...])
    codes += (dot_t(third, at_dir) + dot_t(second, at_dir)) + dot_t(first, at_dir)
    for o in range(8):
        codes_ref[8 * o : 8 * o + 8, :] = jnp.broadcast_to(codes[o : o + 1], (8, 128))
    line = iota((8, NT), 0)
    place_ref[...] = jnp.where(
        line == 0, owner * (8 * 3 * CAP) + rank, jnp.where(line == 1, owner, rank)
    )


def hist_kernel(place_ref, count_ref, pix_ref, pol_ref, out_ref):
    out_ref[...] = jnp.zeros_like(out_ref)
    wide = (16, SB)
    line = iota(wide, 0)
    upper = jnp.where(line < 8, 2 * line, 2 * line - 15).astype(jnp.int16)
    one = jnp.ones(wide, BF)
    zero = jnp.zeros(wide, BF)
    position = iota((1, SB), 1)

    def group(g, carry):
        base = pl.multiple_of(g * 16, 16)
        for r in range(16):
            pixel = pix_ref[pl.ds(base + r, 1), :]
            high = jnp.where(position < count_ref[0, base + r], pixel >> 6, -1)
            high = jnp.broadcast_to(high, wide).astype(jnp.int16)
            low = jnp.broadcast_to(pixel & 63, wide).astype(jnp.int16)
            cos_part = jnp.broadcast_to(pol_ref[0, pl.ds(base, 16), :][r : r + 1], wide)
            sin_part = jnp.broadcast_to(pol_ref[1, pl.ds(base, 16), :][r : r + 1], wide)
            right = jnp.concatenate(
                [jnp.where(low == (line + 16 * q).astype(jnp.int16), one, zero) for q in range(4)],
                axis=0,
            )
            hit = high == upper
            left = jnp.concatenate([jnp.where(hit, w, zero) for w in (one, cos_part, sin_part)], axis=0)
            hits = dot_t(left, right)
            start = place_ref[0, base + r]
            for c in range(3):
                both = jnp.concatenate([hits[16 * c : 16 * c + 8], hits[16 * c + 8 : 16 * c + 16]], axis=1)
                out_ref[pl.ds(start + CAP * c, 8, stride=3 * CAP), :] = both
        return carry

    lax.fori_loop(0, NT // 16, group, 0)


def bin_kernel(hits_ref, pick_ref, dir_ref, out_ref):
    pick = pick_ref[...]
    for c in range(3):
        part = hits_ref[:, CAP * c : CAP * c + CAP, :].reshape(PEERS * CAP, 128) * dir_ref[...]
        sums = dot(pick, jnp.concatenate(pieces(part), axis=1))
        total = (sums[:, 256:] + sums[:, 128:256]) + sums[:, :128]
        out_ref[:, ROWS * c : ROWS * c + ROWS, :] = total.reshape(NZ, ROWS, 128)


def solve_kernel(parts_ref, inverse_ref, out_ref):
    binned = []
    for c in range(3):
        total = parts_ref[0, ROWS * c : ROWS * c + ROWS, :]
        for z in range(1, NZ):
            total = total + parts_ref[z, ROWS * c : ROWS * c + ROWS, :]
        binned.append(total)
    first, second, third = binned
    inv = [inverse_ref[e] for e in range(6)]
    mapped = jnp.concatenate(
        [
            inv[0] * first + inv[1] * second + inv[2] * third,
            inv[1] * first + inv[3] * second + inv[4] * third,
            inv[2] * first + inv[4] * second + inv[5] * third,
        ],
        axis=0,
    )
    for z in range(NZ):
        out_ref[z] = mapped


def correct_kernel(hits_ref, pick_ref, mapped_ref, out_ref):
    pick = pick_ref[...]
    total = None
    for c in range(3):
        maps = mapped_ref[:, ROWS * c : ROWS * c + ROWS, :].reshape(POWN, 128)
        rows = dot(pick, jnp.concatenate(pieces(maps), axis=1))
        rows = (rows[:, 256:] + rows[:, 128:256]) + rows[:, :128]
        term = rows * hits_ref[:, CAP * c : CAP * c + CAP, :].reshape(PEERS * CAP, 128)
        total = term if total is None else total + term
    out_ref[:, 0:CAP] = jnp.sum(total.reshape(PEERS, CAP, 128), axis=-1)
    out_ref[:, CAP:] = jnp.zeros((PEERS, 128 - CAP), F32)


def lanes(values):
    lane = iota((1, 128), 1)
    out = jnp.zeros((1, 128), F32)
    for i, value in enumerate(values):
        out = jnp.where(lane == i, value, out)
    return out


def image_kernel(back_ref, place_ref, count_ref, dir_ref, res_ref, sums_ref, image_ref):
    table = jnp.sum(back_ref[...].reshape(8, 8, 128), axis=1)
    owner_hot = (iota((8, NT), 0) == place_ref[1:2]).astype(F32)
    rank_hot = (iota((128, NT), 0) == place_ref[2:3]).astype(F32).astype(BF)
    first, second, third = pieces(table)
    rows = (dot(third, rank_hot) + dot(second, rank_hot)) + dot(first, rank_hot)
    correction = jnp.sum(rows * owner_hot, axis=0, keepdims=True)
    counts = count_ref[...].astype(F32)
    direction = dir_ref[...]
    resid = res_ref[...]
    image = (counts * direction - correction) / SB
    scaled = SB * resid / counts
    peak = jnp.max(jnp.abs(image), axis=1, keepdims=True)
    unit = image / jnp.where(peak > 0, peak, 1.0)
    row = lanes(
        [
            jnp.sum(resid * scaled, axis=1, keepdims=True),
            jnp.sum(direction * image, axis=1, keepdims=True),
            jnp.sum(unit * scaled, axis=1, keepdims=True),
            jnp.sum(unit * (SB * unit / counts), axis=1, keepdims=True),
            peak,
        ]
    )
    sums_ref[...] = jnp.broadcast_to(row, (PEERS, 128))
    image_ref[...] = image


def merge(rows):
    peaks = rows[:, 4:5]
    peak = jnp.max(peaks, axis=0, keepdims=True)
    ratio = peaks / jnp.where(peak > 0, peak, 1.0)
    total = lambda v: jnp.sum(v, axis=0, keepdims=True)
    return [
        total(rows[:, 0:1]),
        total(rows[:, 1:2]),
        total(rows[:, 2:3] * ratio),
        total(rows[:, 3:4] * ratio * ratio),
        peak,
    ]


def merge_kernel(rows_ref, out_ref):
    out_ref[...] = jnp.broadcast_to(lanes(merge(rows_ref[...])), (NZ, 128))


def step_kernel(rows_ref, amp_ref, res_ref, dir_ref, count_ref, image_ref, amp_out, res_out, dir_out):
    res_norm, curvature, cross, square, peak = merge(rows_ref[...])
    step = res_norm / curvature
    reach = step * peak
    norm_next = (res_norm - 2.0 * reach * cross) + reach * (reach * square)
    direction = dir_ref[...]
    residual_next = res_ref[...] - step * image_ref[...]
    scaled_next = SB * residual_next / count_ref[...].astype(F32)
    amp_out[...] = amp_ref[...] + step * direction
    res_out[...] = residual_next
    dir_out[...] = scaled_next + norm_next / res_norm * direction


def call(body, out_shape, in_specs):
    out_specs = jax.tree.map(lambda _: VMEM, out_shape)
    return pl.pallas_call(
        body, out_shape=out_shape, in_specs=in_specs, out_specs=out_specs, compiler_params=PARAMS
    )


def exchange(value, axes):
    return lax.all_to_all(value, axes, split_axis=0, concat_axis=0, tiled=True)


def local(amplitudes, residual, direction, pointing, pol_weights, counts, tile_patch, patch_slot, inv_hits):
    codes, place = call(
        route_kernel, (shape(PEERS, 128), shape(8, NT, dtype=jnp.int32)), [VMEM] * 3
    )(tile_patch, patch_slot[None], direction)
    codes = exchange(codes, GROUP)
    hits = call(hist_kernel, shape(PEERS * 3 * CAP, 128), [SMEM, SMEM, VMEM, VMEM])(
        place, counts, pointing[0], pol_weights[:, 0]
    )
    hits = exchange(hits.reshape(PEERS, 3 * CAP, 128), GROUP)
    slot_code = codes[:, :CAP].reshape(-1)
    slot_dir = codes[:, CAP : 2 * CAP].reshape(-1)
    names = jnp.arange(1, POWN + 1, dtype=jnp.int32).astype(F32)
    to_map = (names[:, None] == slot_code[None, :]).astype(BF)
    from_map = (slot_code[:, None] == names[None, :]).astype(BF)
    dir_rows = jnp.broadcast_to(slot_dir[:, None], (PEERS * CAP, 128))
    z = lax.axis_index("z")
    part = lax.axis_index("x") * 2 + lax.axis_index("c")
    own = lax.dynamic_slice(inv_hits, (0, z * (ROWS * PP)), (6, ROWS * PP)).reshape(6, ROWS, 8, 128)
    own = lax.dynamic_index_in_dim(own, part, axis=2, keepdims=False)
    binned = call(bin_kernel, shape(NZ, 3 * ROWS, 128), [VMEM] * 3)(hits, to_map, dir_rows)
    mapped = call(solve_kernel, shape(NZ, 3 * ROWS, 128), [VMEM] * 2)(exchange(binned, "z"), own)
    partial = call(correct_kernel, shape(PEERS, 128), [VMEM] * 3)(hits, from_map, exchange(mapped, "z"))
    sums, image = call(image_kernel, (shape(PEERS, 128), shape(1, NT)), [VMEM] * 5)(
        exchange(partial, GROUP), place, counts, direction, residual
    )
    sums = call(merge_kernel, shape(NZ, 128), [VMEM])(exchange(sums, GROUP))
    return call(step_kernel, (shape(1, NT),) * 3, [VMEM] * 6)(
        exchange(sums, "z"), amplitudes, residual, direction, counts, image
    )


def solution(mesh):
    fine = Mesh(mesh.devices.reshape(8, NZ, 4, 2), ("det", "z", "x", "c"))
    span = ("z", "x", "c")
    flat = P("det", span)
    in_specs = (
        flat,
        flat,
        flat,
        P("det", span, None),
        P(None, "det", span, None),
        flat,
        flat,
        P(),
        P(None, "det"),
    )
    return jax.shard_map(local, mesh=fine, in_specs=in_specs, out_specs=(flat,) * 3, check_vma=False)
```

```python
import functools
import jax
import jax.numpy as jnp
from jax import lax
from jax.experimental import pallas as pl
from jax.experimental.pallas import tpu as pltpu
from jax.sharding import Mesh, PartitionSpec as P

SB = 4096
PP = 1024
NT = 64
POWN = 96
CAP = 16
NPATCH = 768
NZ = 12
ROWS = POWN // NZ
GROUP = ("det", "x", "c")
PEERS = 64
BF = jnp.bfloat16
F32 = jnp.float32
NT_DIMS = (((1,), (1,)), ((), ()))
VMEM = pl.BlockSpec(memory_space=pltpu.VMEM)
SMEM = pl.BlockSpec(memory_space=pltpu.SMEM)
PARAMS = pltpu.CompilerParams(vmem_limit_bytes=32 * 2**20)


def shape(*dims, dtype=F32):
    return jax.ShapeDtypeStruct(dims, dtype)


def iota(dims, axis):
    return lax.broadcasted_iota(jnp.int32, dims, axis)


def pieces(value):
    first = value.astype(BF)
    rest = value - first.astype(F32)
    second = rest.astype(BF)
    third = (rest - second.astype(F32)).astype(BF)
    return first, second, third


def dot(left, right):
    return jnp.dot(left, right, preferred_element_type=F32)


def dot_t(left, right):
    return lax.dot_general(left, right, NT_DIMS, preferred_element_type=F32)


def route_kernel(place_ref, dir_ref, res_ref, count_ref, codes_ref):
    owner, rank, row = place_ref[0:1], place_ref[1:2], place_ref[2:3]
    hot = (iota((8, NT), 0) == owner).astype(F32)
    lane = iota((128, NT), 0)
    codes = jnp.zeros((8, 128), F32)
    values = ((row + 1).astype(F32), dir_ref[...], res_ref[...], count_ref[...].astype(F32))
    for i, value in enumerate(values):
        spot = (lane == rank + CAP * i).astype(F32).astype(BF)
        first, second, third = pieces(hot * value)
        codes += (dot_t(third, spot) + dot_t(second, spot)) + dot_t(first, spot)
    for o in range(8):
        codes_ref[8 * o : 8 * o + 8, :] = jnp.broadcast_to(codes[o : o + 1], (8, 128))


def hist_kernel(patch_ref, slot_ref, count_ref, pix_ref, pol_ref, out_ref, place_ref, used_ref):
    out_ref[...] = jnp.zeros_like(out_ref)
    for o in range(8):
        used_ref[o] = 0
    wide = (16, SB)
    line = iota(wide, 0)
    upper = jnp.where(line < 8, 2 * line, 2 * line - 15).astype(jnp.int16)
    one = jnp.ones(wide, BF)
    zero = jnp.zeros(wide, BF)
    position = iota((1, SB), 1)

    def group(g, carry):
        base = pl.multiple_of(g * 16, 16)
        for r in range(16):
            pixel = pix_ref[pl.ds(base + r, 1), :]
            high = jnp.where(position < count_ref[0, base + r], pixel >> 6, -1)
            high = jnp.broadcast_to(high, wide).astype(jnp.int16)
            low = jnp.broadcast_to(pixel & 63, wide).astype(jnp.int16)
            cos_part = jnp.broadcast_to(pol_ref[0, pl.ds(base, 16), :][r : r + 1], wide)
            sin_part = jnp.broadcast_to(pol_ref[1, pl.ds(base, 16), :][r : r + 1], wide)
            right = jnp.concatenate(
                [jnp.where(low == (line + 16 * q).astype(jnp.int16), one, zero) for q in range(4)],
                axis=0,
            )
            hit = high == upper
            left = jnp.concatenate([jnp.where(hit, w, zero) for w in (one, cos_part, sin_part)], axis=0)
            hits = dot_t(left, right)
            slot = slot_ref[patch_ref[0, base + r]]
            owner = (slot * 683) >> 16
            rank = used_ref[owner]
            used_ref[owner] = rank + 1
            place_ref[0, base + r] = owner
            place_ref[1, base + r] = rank
            place_ref[2, base + r] = slot - POWN * owner
            start = owner * (8 * 3 * CAP) + rank
            for c in range(3):
                both = jnp.concatenate([hits[16 * c : 16 * c + 8], hits[16 * c + 8 : 16 * c + 16]], axis=1)
                out_ref[pl.ds(start + CAP * c, 8, stride=3 * CAP), :] = both
        return carry

    lax.fori_loop(0, NT // 16, group, 0)


def bin_kernel(hits_ref, pick_ref, dir_ref, out_ref):
    pick = pick_ref[...]
    for c in range(3):
        part = hits_ref[:, CAP * c : CAP * c + CAP, :].reshape(PEERS * CAP, 128) * dir_ref[...]
        sums = dot(pick, jnp.concatenate(pieces(part), axis=1))
        total = (sums[:, 256:] + sums[:, 128:256]) + sums[:, :128]
        out_ref[:, ROWS * c : ROWS * c + ROWS, :] = total.reshape(NZ, ROWS, 128)


def solve_kernel(parts_ref, inverse_ref, out_ref):
    binned = []
    for c in range(3):
        total = parts_ref[0, ROWS * c : ROWS * c + ROWS, :]
        for z in range(1, NZ):
            total = total + parts_ref[z, ROWS * c : ROWS * c + ROWS, :]
        binned.append(total)
    first, second, third = binned
    inv = [inverse_ref[e] for e in range(6)]
    mapped = jnp.concatenate(
        [
            inv[0] * first + inv[1] * second + inv[2] * third,
            inv[1] * first + inv[3] * second + inv[4] * third,
            inv[2] * first + inv[4] * second + inv[5] * third,
        ],
        axis=0,
    )
    for z in range(NZ):
        out_ref[z] = mapped


def correct_kernel(hits_ref, pick_ref, mapped_ref, out_ref):
    pick = pick_ref[...]
    total = None
    for c in range(3):
        maps = mapped_ref[:, ROWS * c : ROWS * c + ROWS, :].reshape(POWN, 128)
        rows = dot(pick, jnp.concatenate(pieces(maps), axis=1))
        rows = (rows[:, 256:] + rows[:, 128:256]) + rows[:, :128]
        term = rows * hits_ref[:, CAP * c : CAP * c + CAP, :].reshape(PEERS * CAP, 128)
        total = term if total is None else total + term
    partial = fold(jnp.sum(total.reshape(PEERS, CAP, 128), axis=-1))
    for p in range(8):
        out_ref[p] = partial


def fold(rows):
    return jnp.concatenate([rows[8 * j : 8 * j + 8] for j in range(8)], axis=1)


def lanes(values, first):
    lane = iota((1, 128), 1)
    out = jnp.zeros((1, 128), F32)
    for i, value in enumerate(values):
        out = jnp.where(lane == first + i, value, out)
    return out


def total(value):
    return jnp.sum(jnp.sum(value, axis=0, keepdims=True), axis=1, keepdims=True)


def image_kernel(part_ref, codes_ref, parts_ref, out_ref):
    correction = parts_ref[0]
    for p in range(1, 8):
        correction = correction + parts_ref[p]
    code, direction, resid, counts = [fold(codes_ref[:, CAP * i : CAP * i + CAP]) for i in range(4)]
    counts = jnp.where(code > 0, counts, 1.0)
    image = jnp.where(code > 0, (counts * direction - correction) / SB, 0.0)
    scaled = SB * resid / counts
    size = jnp.abs(image)
    peak = jnp.max(jnp.max(size, axis=0, keepdims=True), axis=1, keepdims=True)
    unit = image / jnp.where(peak > 0, peak, 1.0)
    sums = lanes(
        [
            total(resid * scaled),
            total(direction * image),
            total(unit * scaled),
            total(unit * (SB * unit / counts)),
            peak,
        ],
        CAP,
    )
    mine = iota((8, 128), 0) == part_ref[0]
    row = jnp.sum(jnp.where(mine, correction, 0.0), axis=0, keepdims=True)
    lane = iota((1, 128), 1)
    for y in range(8):
        piece = jnp.concatenate([row[:, CAP * y : CAP * y + CAP], jnp.zeros((1, 128 - CAP), F32)], axis=1)
        out_ref[y : y + 1, :] = jnp.where(lane < CAP, piece, sums)


def merge(rows):
    lead = [row[:, CAP + i : CAP + i + 1] for row in rows for i in range(5)]
    rows = [lead[5 * k : 5 * k + 5] for k in range(len(rows))]
    peak = functools.reduce(jnp.maximum, [row[4] for row in rows])
    safe = jnp.where(peak > 0, peak, 1.0)
    out = None
    for row in rows:
        ratio = row[4] / safe
        terms = [row[0], row[1], row[2] * ratio, row[3] * ratio * ratio]
        out = terms if out is None else [a + b for a, b in zip(out, terms)]
    return out + [peak]


def merge_kernel(rows_ref, out_ref):
    row = lanes(merge([rows_ref[y : y + 1] for y in range(8)]), CAP)
    for z in range(NZ):
        out_ref[z] = row


def step_kernel(
    rows_ref, back_ref, place_ref, amp_ref, res_ref, dir_ref, count_ref, amp_out, res_out, dir_out
):
    owner_hot = (iota((8, NT), 0) == place_ref[0:1]).astype(F32)
    rank_hot = (iota((128, NT), 0) == place_ref[1:2]).astype(F32).astype(BF)
    first, second, third = pieces(back_ref[...])
    rows = (dot(third, rank_hot) + dot(second, rank_hot)) + dot(first, rank_hot)
    correction = jnp.sum(rows * owner_hot, axis=0, keepdims=True)
    counts = count_ref[...].astype(F32)
    direction = dir_ref[...]
    image = (counts * direction - correction) / SB
    res_norm, curvature, cross, square, peak = merge([rows_ref[z] for z in range(NZ)])
    step = res_norm / curvature
    reach = step * peak
    norm_next = (res_norm - 2.0 * reach * cross) + reach * (reach * square)
    residual_next = res_ref[...] - step * image
    scaled_next = SB * residual_next / counts
    amp_out[...] = amp_ref[...] + step * direction
    res_out[...] = residual_next
    dir_out[...] = scaled_next + norm_next / res_norm * direction


def call(body, out_shape, in_specs, out_specs=None, scratch=()):
    out_specs = jax.tree.map(lambda _: VMEM, out_shape) if out_specs is None else out_specs
    return pl.pallas_call(
        body,
        out_shape=out_shape,
        in_specs=in_specs,
        out_specs=out_specs,
        scratch_shapes=scratch,
        compiler_params=PARAMS,
    )


def exchange(value, axes):
    return lax.all_to_all(value, axes, split_axis=0, concat_axis=0, tiled=True)


def local(amplitudes, residual, direction, pointing, pol_weights, counts, tile_patch, patch_slot, inv_hits):
    hits, place = call(
        hist_kernel,
        (shape(PEERS * 3 * CAP, 128), shape(3, NT, dtype=jnp.int32)),
        [SMEM, SMEM, SMEM, VMEM, VMEM],
        (VMEM, SMEM),
        [pltpu.SMEM((8,), jnp.int32)],
    )(tile_patch, patch_slot, counts, pointing[0], pol_weights[:, 0])
    hits = exchange(hits.reshape(PEERS, 3 * CAP, 128), GROUP)
    codes = call(route_kernel, shape(PEERS, 128), [VMEM] * 4)(place, direction, residual, counts)
    codes = exchange(codes, GROUP)
    slot_code = codes[:, :CAP].reshape(-1)
    slot_dir = codes[:, CAP : 2 * CAP].reshape(-1)
    names = jnp.arange(1, POWN + 1, dtype=jnp.int32).astype(F32)
    to_map = (names[:, None] == slot_code[None, :]).astype(BF)
    from_map = (slot_code[:, None] == names[None, :]).astype(BF)
    dir_rows = jnp.broadcast_to(slot_dir[:, None], (PEERS * CAP, 128))
    z = lax.axis_index("z")
    part = lax.axis_index("x") * 2 + lax.axis_index("c")
    own = lax.dynamic_slice(inv_hits, (0, z * (ROWS * PP)), (6, ROWS * PP)).reshape(6, ROWS, 8, 128)
    own = lax.dynamic_index_in_dim(own, part, axis=2, keepdims=False)
    binned = call(bin_kernel, shape(NZ, 3 * ROWS, 128), [VMEM] * 3)(hits, to_map, dir_rows)
    mapped = call(solve_kernel, shape(NZ, 3 * ROWS, 128), [VMEM] * 2)(exchange(binned, "z"), own)
    partial = call(correct_kernel, shape(8, 8, 128), [VMEM] * 3)(hits, from_map, exchange(mapped, "z"))
    back = call(image_kernel, shape(8, 128), [SMEM, VMEM, VMEM])(
        part[None], codes, exchange(partial, ("x", "c"))
    )
    back = exchange(back, "det")
    sums = call(merge_kernel, shape(NZ, 1, 128), [VMEM])(back)
    return call(step_kernel, (shape(1, NT),) * 3, [VMEM] * 7)(
        exchange(sums, "z"), back, place, amplitudes, residual, direction, counts
    )


def solution(mesh):
    fine = Mesh(mesh.devices.reshape(8, NZ, 4, 2), ("det", "z", "x", "c"))
    span = ("z", "x", "c")
    flat = P("det", span)
    in_specs = (
        flat,
        flat,
        flat,
        P("det", span, None),
        P(None, "det", span, None),
        flat,
        flat,
        P(),
        P(None, "det"),
    )
    return jax.shard_map(local, mesh=fine, in_specs=in_specs, out_specs=(flat,) * 3, check_vma=False)
```
